32 devices in a mesh: tm: 16 (over z, y, core), mom: 2 (over x).
Axes of the slice: x: 2, y: 2, z: 4, core: 2. Of those that a mesh axis runs over, the one named last changes fastest.
Arguments:
- sink_solutions: bfloat16 [16, 2, 512, 512], P('tm'), may hold values from -0.44921875 to 0.44921875
- noise_sources: bfloat16 [16, 2, 512, 512], P('tm'), may hold values from -0.44921875 to 0.44921875
- elementals: bfloat16 [2, 16, 2, 128, 128], P('mom', 'tm'), may hold values from -0.375 to 0.375
- pairs: int32 [2, 2], P('mom'), may hold values from 0 to 1
Outputs:
- blocks: bfloat16 [16, 4, 2, 2, 512, 512], P('tm', None, 'mom')
The draws below stay inside these ranges and needn't reach their ends.
Inputs may be any that keep to these rules, and one draw needn't show every extreme that they name: `pairs`: entries are operator indices.
All inputs are finite; a program needn't handle non-finite values.
Results may differ from the reference program's by a relative error of at most 0.007.
Values may be sent and summed in bfloat16 or wider, within the bound.
A program may use at most 64 MiB of HBM per device.

```python
import jax
import jax.numpy as jnp
from jax import lax

NEV = 128
EIGEN_SPIN_SIZE = 512
DILUTION_INDICES = 512
NSEP = 4
TIME_SLICES = 16
NOP = 2
NPAIR = 2


def with_ends(entries, stream_key, low, high):
    spot = [jax.random.randint(jax.random.fold_in(stream_key, axis), (), 0, length) for axis, length in enumerate(entries.shape)]
    widest = entries.shape.index(max(entries.shape))
    neighbour = spot[:widest] + [(spot[widest] + 1) % entries.shape[widest]] + spot[widest + 1:]
    return entries.at[tuple(spot)].set(low).at[tuple(neighbour)].set(high)


def levels(stream_key, dims, split, smallest, high):
    level, own = 1.0, jax.random.fold_in(stream_key, 6)
    for dim, parts in split:
        heights = jnp.exp(jax.random.uniform(jax.random.fold_in(own, dim), (parts,), jnp.float32, smallest / len(split), high / len(split)))
        level = level * jnp.repeat(heights, dims[dim] // parts).reshape([-1 if axis == dim else 1 for axis in range(len(dims))])
    return level


def normal_values(key, extent, spread, reach, split=(), kind=jnp.bfloat16):
    entries = spread * jax.random.normal(key, extent, jnp.float32)
    if split:
        entries = entries * levels(key, extent, split, -0.22, 0.18)
    return jnp.clip(entries, -reach, reach).astype(kind)


def setup_inputs(seed: int = 0) -> dict:
    key_list = jax.random.split(jax.random.key(seed), 5)
    return {
        "sink_solutions": normal_values(key_list[0], (TIME_SLICES, 2, DILUTION_INDICES, EIGEN_SPIN_SIZE), 0.075, 0.44921875, ((0, 16),)),
        "noise_sources": normal_values(key_list[1], (TIME_SLICES, 2, DILUTION_INDICES, EIGEN_SPIN_SIZE), 0.075, 0.44921875, ((0, 16),)),
        "elementals": normal_values(key_list[2], (NOP, TIME_SLICES, 2, NEV, NEV), (2 * NEV) ** -0.5, 0.375, ((0, 2), (1, 16))),
        "pairs": with_ends(jax.random.randint(key_list[3], (NPAIR, 2), 0, NOP), jax.random.fold_in(key_list[3], 1), 0, NOP - 1).astype(jnp.int32),
    }


def transpose_product(left_mat, right_mat):
    return lax.dot_general(left_mat, right_mat, (((1,), (1,)), ((), ())), preferred_element_type=jnp.float32)


def complex_product(left_mat, right_mat):
    real_part = jnp.dot(left_mat[0], right_mat[0], preferred_element_type=jnp.float32) - jnp.dot(left_mat[1], right_mat[1], preferred_element_type=jnp.float32)
    imag_part = jnp.dot(left_mat[0], right_mat[1], preferred_element_type=jnp.float32) + jnp.dot(left_mat[1], right_mat[0], preferred_element_type=jnp.float32)
    return jnp.stack([real_part, imag_part])


def meson_function(sink_piece, noise_part, elemental):
    dilution_rows = sink_piece.shape[1]
    total_width = sink_piece.shape[2]
    eigenvector_count = elemental.shape[1]
    spinor_rows = sink_piece.reshape(2, dilution_rows * (total_width // eigenvector_count), eigenvector_count)
    applied_real = transpose_product(spinor_rows[0], elemental[0]) - transpose_product(spinor_rows[1], elemental[1])
    applied_imaginary = transpose_product(spinor_rows[0], elemental[1]) + transpose_product(spinor_rows[1], elemental[0])
    applied_result = jnp.stack([applied_real, applied_imaginary]).reshape(2, dilution_rows, total_width).astype(jnp.bfloat16)
    meson_re = transpose_product(noise_part[0], applied_result[0]) + transpose_product(noise_part[1], applied_result[1])
    meson_im = transpose_product(noise_part[0], applied_result[1]) - transpose_product(noise_part[1], applied_result[0])
    return jnp.stack([meson_re, meson_im]).astype(jnp.bfloat16)


def reference(sink_solutions, noise_sources, elementals, pairs):
    slice_times = jnp.arange(TIME_SLICES, dtype=jnp.int32)

    def mesons_at(slice_time):
        return lax.map(lambda operator: meson_function(sink_solutions[slice_time], noise_sources[slice_time], elementals[operator, slice_time]), jnp.arange(NOP, dtype=jnp.int32))

    mesons = lax.map(mesons_at, slice_times)

    def blocks_at(source_time):
        source_side = mesons[source_time][pairs[:, 1]]
        results = []
        for separation in range(1, NSEP + 1):
            later_time = ((source_time + separation) % TIME_SLICES).astype(jnp.int32)
            sink_side = mesons[later_time][pairs[:, 0]]
            results.append(jax.vmap(complex_product)(sink_side, source_side).astype(jnp.bfloat16))
        return jnp.stack(results)

    return lax.map(blocks_at, slice_times)
```

```python
import functools

import jax
import jax.numpy as jnp
from jax import lax
from jax.experimental import pallas as pl
from jax.experimental.pallas import tpu as pltpu
from jax.sharding import PartitionSpec as P

NSEP = 4
MESH = pl.DeviceIdType.MESH
CHUNKS = 8


def dot(left, right):
    return jnp.dot(left, right, preferred_element_type=jnp.float32)


def kernel(
    n_times, n_mom, chunks,
    sink_hbm, noise_hbm, elem_hbm, pairs_ref, out_hbm,
    sink, noise, elems, weights, own, source, recv, staged,
    load_sem, elem_send, elem_recv, send_sem, recv_sem, out_sem,
):
    time = lax.axis_index("tm")
    mom = lax.axis_index("mom")
    odd = lax.rem(time, 2)
    upper = lax.rem(time // 2, 2)
    sibling = time + 1 - 2 * odd
    across = time + 2 - 4 * upper
    before = lax.rem(time + n_times - 4, n_times)
    after = lax.rem(time + 4, n_times)

    width = sink.shape[2]
    dil = sink.shape[1]
    ops = elem_hbm.shape[0]
    nev = elem_hbm.shape[3]
    spins = width // nev
    rows = dil // chunks

    own_elem = pltpu.make_async_copy(
        elem_hbm.at[:, 0], elems.at[pl.ds(mom * ops, ops)], load_sem.at[0]
    )
    own_elem.start()
    sink_load = pltpu.make_async_copy(sink_hbm.at[0], sink, load_sem.at[1])
    sink_load.start()
    noise_loads = [
        pltpu.make_async_copy(
            noise_hbm.at[0, part], noise.at[:, pl.ds(part * width, width)], load_sem.at[2 + part]
        )
        for part in range(2)
    ]
    for load in noise_loads:
        load.start()

    barrier = pltpu.get_barrier_semaphore()
    mom_peers = [lax.rem(mom + step, n_mom) for step in range(1, n_mom)]
    for peer in mom_peers:
        pl.semaphore_signal(barrier, inc=1, device_id=(time, peer), device_id_type=MESH)
    for peer in (sibling, across, before, after):
        pl.semaphore_signal(barrier, inc=1, device_id=(peer, mom), device_id_type=MESH)
    pl.semaphore_wait(barrier, n_mom - 1 + 4)

    elem_sends = []
    for step, peer in enumerate(mom_peers):
        send = pltpu.make_async_remote_copy(
            src_ref=elem_hbm.at[:, 0],
            dst_ref=elems.at[pl.ds(mom * ops, ops)],
            send_sem=elem_send.at[step],
            recv_sem=elem_recv.at[step],
            device_id=(time, peer),
            device_id_type=MESH,
        )
        send.start()
        elem_sends.append(send)
    own_elem.wait()
    sink_load.wait()
    for send in elem_sends:
        send.wait_recv()
    for load in noise_loads:
        load.wait()

    def fill_weights(which):
        chosen = elems[pairs_ref[0, which]]
        real, imag = chosen[0], chosen[1]
        left = jnp.concatenate(
            [jnp.concatenate([real, -imag], axis=1), jnp.concatenate([imag, real], axis=1)], axis=0
        )
        for spin in range(spins):
            cols = pl.ds(spin * nev, nev)
            right = jnp.concatenate([sink[0, :, cols], sink[1, :, cols]], axis=1)
            applied = lax.dot_general(
                left, right, (((1,), (1,)), ((), ())), preferred_element_type=jnp.float32
            ).astype(jnp.bfloat16)
            ap_re, ap_im = applied[:nev], applied[nev:]
            upper_rows = pl.ds(spin * nev, nev)
            lower_rows = pl.ds(width + spin * nev, nev)
            weights[upper_rows, :dil] = ap_re
            weights[upper_rows, dil:] = ap_im
            weights[lower_rows, :dil] = ap_im
            weights[lower_rows, dil:] = -ap_re

    def copy(src, slot, chunk, lane, target):
        at = pl.ds(pl.multiple_of(chunk * rows, rows), rows)
        return pltpu.make_async_remote_copy(
            src_ref=src.at[at],
            dst_ref=recv.at[slot, at],
            send_sem=send_sem.at[lane, chunk],
            recv_sem=recv_sem.at[slot, chunk],
            device_id=(target, mom),
            device_id_type=MESH,
        )

    def arrived(slot, chunk):
        copy(own, slot, chunk, 0, before).wait_recv()

    fill_weights(0)

    def make_own(chunk, carry):
        at = pl.ds(pl.multiple_of(chunk * rows, rows), rows)
        own[at, :] = dot(noise[at, :], weights[...]).astype(jnp.bfloat16)
        copy(own, 3, chunk, 0, before).start()

        @pl.when(upper == 1)
        def _():
            copy(own, 1, chunk, 1, across).start()

        @pl.when(odd == 1)
        def _():
            copy(own, 0, chunk, 2, sibling).start()

        return carry

    lax.fori_loop(0, chunks, make_own, 0)

    fill_weights(1)
    half = dil // 2

    def make_source(part, carry):
        at = pl.ds(pl.multiple_of(part * half, half), half)
        lower = pl.ds(pl.multiple_of(dil + part * half, half), half)
        meson = dot(noise[at, :], weights[...]).astype(jnp.bfloat16)
        re, im = meson[:, :dil], meson[:, dil:]
        source[at, :dil] = re
        source[at, dil:] = im
        source[lower, :dil] = -im
        source[lower, dil:] = re
        return carry

    lax.fori_loop(0, 2, make_source, 0)

    def finish(slot, chunk):
        at = pl.ds(pl.multiple_of(chunk * rows, rows), rows)
        block = dot(recv[slot, at, :], source[...]).astype(jnp.bfloat16)
        staged[slot, 0, at, :] = block[:, :dil]
        staged[slot, 1, at, :] = block[:, dil:]
        pltpu.make_async_copy(
            staged.at[slot, :, at], out_hbm.at[0, slot, 0, :, at], out_sem
        ).start()

    def step(chunk, carry):
        arrived(3, chunk)

        @pl.when(upper == 0)
        def _():
            copy(recv.at[3], 1, chunk, 1, across).start()

        @pl.when(odd == 0)
        def _():
            copy(recv.at[3], 2, chunk, 2, sibling).start()

        arrived(1, chunk)

        @pl.when(odd == 0)
        def _():
            copy(recv.at[1], 0, chunk, 3, sibling).start()

        @pl.when(odd == 1)
        def _():
            copy(recv.at[1], 2, chunk, 3, sibling).start()

        finish(3, chunk)
        finish(1, chunk)
        arrived(0, chunk)
        finish(0, chunk)
        arrived(2, chunk)
        finish(2, chunk)
        return carry

    lax.fori_loop(0, chunks, step, 0)

    for send in elem_sends:
        send.wait_send()

    def drain(chunk, carry):
        for lane in range(4):
            copy(own, 0, chunk, lane, before).wait_send()
        return carry

    lax.fori_loop(0, chunks, drain, 0)
    pltpu.make_async_copy(staged, out_hbm.at[0, :, 0], out_sem).wait()


def local(n_times, n_mom, sink_solutions, noise_sources, elementals, pairs):
    _, _, dil, width = sink_solutions.shape
    ops, _, _, nev, _ = elementals.shape
    chunks = CHUNKS
    bf16 = jnp.bfloat16
    flops = 2 * 2 * 4 * dil * width * (nev + dil) + NSEP * 2 * 4 * dil**3
    return pl.pallas_call(
        functools.partial(kernel, n_times, n_mom, chunks),
        out_shape=jax.ShapeDtypeStruct((1, NSEP, 1, 2, dil, dil), bf16),
        in_specs=[
            pl.BlockSpec(memory_space=pl.ANY),
            pl.BlockSpec(memory_space=pl.ANY),
            pl.BlockSpec(memory_space=pl.ANY),
            pl.BlockSpec(memory_space=pltpu.SMEM),
        ],
        out_specs=pl.BlockSpec(memory_space=pl.ANY),
        scratch_shapes=[
            pltpu.VMEM((2, dil, width), bf16),
            pltpu.VMEM((dil, 2 * width), bf16),
            pltpu.VMEM((n_mom * ops, 2, nev, nev), bf16),
            pltpu.VMEM((2 * width, 2 * dil), bf16),
            pltpu.VMEM((dil, 2 * dil), bf16),
            pltpu.VMEM((2 * dil, 2 * dil), bf16),
            pltpu.VMEM((NSEP, dil, 2 * dil), bf16),
            pltpu.VMEM((NSEP, 2, dil, dil), bf16),
            pltpu.SemaphoreType.DMA((4,)),
            pltpu.SemaphoreType.DMA((max(n_mom - 1, 1),)),
            pltpu.SemaphoreType.DMA((max(n_mom - 1, 1),)),
            pltpu.SemaphoreType.DMA((4, chunks)),
            pltpu.SemaphoreType.DMA((4, chunks)),
            pltpu.SemaphoreType.DMA,
        ],
        compiler_params=pltpu.CompilerParams(
            collective_id=0, has_side_effects=True, vmem_limit_bytes=40 * 1024 * 1024
        ),
        cost_estimate=pl.CostEstimate(
            flops=flops, bytes_accessed=2 * (4 * dil * width + 8 * dil * dil), transcendentals=0
        ),
    )(sink_solutions, noise_sources, elementals, pairs)


def solution(mesh):
    return jax.shard_map(
        functools.partial(local, mesh.shape["tm"], mesh.shape["mom"]),
        mesh=mesh,
        in_specs=(
            P("tm", None, None, None),
            P("tm", None, None, None),
            P("mom", "tm", None, None, None),
            P("mom", None),
        ),
        out_specs=P("tm", None, "mom", None, None, None),
        check_vma=False,
    )
```

```python
import functools

import jax
import jax.numpy as jnp
from jax import lax
from jax.experimental import pallas as pl
from jax.experimental.pallas import tpu as pltpu
from jax.sharding import PartitionSpec as P

NSEP = 4
MESH = pl.DeviceIdType.MESH
CHUNKS = 16


def dot(left, right):
    return jnp.dot(left, right, preferred_element_type=jnp.float32)


def kernel(
    n_times, n_mom, chunks,
    sink_hbm, noise_hbm, elem_hbm, pairs_hbm, out_hbm,
    pairs_ref, sink, noise, elems, weights, own, source, recv, staged,
    load_sem, elem_send, elem_recv, send_sem, recv_sem, out_sem,
):
    time = lax.axis_index("tm")
    mom = lax.axis_index("mom")
    odd = lax.rem(time, 2)
    upper = lax.rem(time // 2, 2)
    sibling = time + 1 - 2 * odd
    across = time + 2 - 4 * upper
    before = lax.rem(time + n_times - 4, n_times)
    after = lax.rem(time + 4, n_times)

    width = sink.shape[2]
    dil = sink.shape[1]
    ops = elem_hbm.shape[0]
    nev = elem_hbm.shape[3]
    spins = width // nev
    rows = dil // chunks

    own_elem = pltpu.make_async_copy(
        elem_hbm.at[:, 0], elems.at[pl.ds(mom * ops, ops)], load_sem.at[0]
    )
    own_elem.start()
    pairs_load = pltpu.make_async_copy(pairs_hbm, pairs_ref, load_sem.at[4])
    pairs_load.start()
    sink_load = pltpu.make_async_copy(sink_hbm.at[0], sink, load_sem.at[1])
    sink_load.start()
    noise_loads = [
        pltpu.make_async_copy(
            noise_hbm.at[0, part], noise.at[:, pl.ds(part * width, width)], load_sem.at[2 + part]
        )
        for part in range(2)
    ]
    for load in noise_loads:
        load.start()

    barrier = pltpu.get_barrier_semaphore()
    mom_peers = [lax.rem(mom + step, n_mom) for step in range(1, n_mom)]
    for peer in mom_peers:
        pl.semaphore_signal(barrier, inc=1, device_id=(time, peer), device_id_type=MESH)
    for peer in (sibling, across, before, after):
        pl.semaphore_signal(barrier, inc=1, device_id=(peer, mom), device_id_type=MESH)
    pl.semaphore_wait(barrier, n_mom - 1 + 4)

    elem_sends = []
    for step, peer in enumerate(mom_peers):
        send = pltpu.make_async_remote_copy(
            src_ref=elem_hbm.at[:, 0],
            dst_ref=elems.at[pl.ds(mom * ops, ops)],
            send_sem=elem_send.at[step],
            recv_sem=elem_recv.at[step],
            device_id=(time, peer),
            device_id_type=MESH,
        )
        send.start()
        elem_sends.append(send)
    own_elem.wait()
    pairs_load.wait()
    sink_load.wait()
    for send in elem_sends:
        send.wait_recv()
    for load in noise_loads:
        load.wait()

    def fill_weights(which):
        chosen = elems[pairs_ref[0, which]]
        real, imag = chosen[0], chosen[1]
        left = jnp.concatenate(
            [jnp.concatenate([real, -imag], axis=1), jnp.concatenate([imag, real], axis=1)], axis=0
        )
        for spin in range(spins):
            cols = pl.ds(spin * nev, nev)
            right = jnp.concatenate([sink[0, :, cols], sink[1, :, cols]], axis=1)
            applied = lax.dot_general(
                left, right, (((1,), (1,)), ((), ())), preferred_element_type=jnp.float32
            ).astype(jnp.bfloat16)
            ap_re, ap_im = applied[:nev], applied[nev:]
            upper_rows = pl.ds(spin * nev, nev)
            lower_rows = pl.ds(width + spin * nev, nev)
            weights[upper_rows, :dil] = ap_re
            weights[upper_rows, dil:] = ap_im
            weights[lower_rows, :dil] = ap_im
            weights[lower_rows, dil:] = -ap_re

    def copy(src, slot, chunk, lane, target):
        at = pl.ds(pl.multiple_of(chunk * rows, rows), rows)
        return pltpu.make_async_remote_copy(
            src_ref=src.at[at],
            dst_ref=recv.at[slot, at],
            send_sem=send_sem.at[lane, chunk],
            recv_sem=recv_sem.at[slot, chunk],
            device_id=(target, mom),
            device_id_type=MESH,
        )

    def arrived(slot, chunk):
        copy(own, slot, chunk, 0, before).wait_recv()

    fill_weights(0)

    def send_own(chunk):
        copy(own, 3, chunk, 0, before).start()

        @pl.when(upper == 1)
        def _():
            copy(own, 1, chunk, 1, across).start()

        @pl.when(odd == 1)
        def _():
            copy(own, 0, chunk, 2, sibling).start()

    tall = 4 * rows

    def make_own(part, carry):
        at = pl.ds(pl.multiple_of(part * tall, tall), tall)
        own[at, :] = dot(noise[at, :], weights[...]).astype(jnp.bfloat16)
        for piece in range(4):
            send_own(part * 4 + piece)
        return carry

    lax.fori_loop(0, dil // tall, make_own, 0)

    def make_source(part):
        at = pl.ds(pl.multiple_of(part * tall, tall), tall)
        lower = pl.ds(pl.multiple_of(dil + part * tall, tall), tall)
        meson = dot(noise[at, :], weights[...]).astype(jnp.bfloat16)
        re, im = meson[:, :dil], meson[:, dil:]
        source[at, :dil] = re
        source[at, dil:] = im
        source[lower, :dil] = -im
        source[lower, dil:] = re

    def forward(chunk):
        arrived(3, chunk)

        @pl.when(upper == 0)
        def _():
            copy(recv.at[3], 1, chunk, 1, across).start()

        @pl.when(odd == 0)
        def _():
            copy(recv.at[3], 2, chunk, 2, sibling).start()

        arrived(1, chunk)

        @pl.when(odd == 0)
        def _():
            copy(recv.at[1], 0, chunk, 3, sibling).start()

        @pl.when(odd == 1)
        def _():
            copy(recv.at[1], 2, chunk, 3, sibling).start()

    pair = 2 * rows

    def finish(part):
        at = pl.ds(pl.multiple_of(part * pair, pair), pair)
        for piece in range(2):
            arrived(0, part * 2 + piece)
            arrived(2, part * 2 + piece)
        later = recv[:, at, :].reshape(NSEP * pair, 2 * dil)
        block = dot(later, source[...]).astype(jnp.bfloat16).reshape(NSEP, pair, 2 * dil)
        staged[:, 0, at, :] = block[:, :, :dil]
        staged[:, 1, at, :] = block[:, :, dil:]
        pltpu.make_async_copy(staged.at[:, :, at], out_hbm.at[0, :, 0, :, at], out_sem).start()

    forward(0)
    fill_weights(1)

    def with_source(part, carry):
        forward(1 + part)
        make_source(part)
        return carry

    lax.fori_loop(0, 4, with_source, 0)

    def with_backlog(part, carry):
        forward(5 + part)
        finish(part)
        return carry

    lax.fori_loop(0, 4, with_backlog, 0)

    def steady(part, carry):
        forward(1 + 2 * part)
        forward(2 + 2 * part)
        finish(part)
        return carry

    lax.fori_loop(4, chunks // 2 - 1, steady, 0)
    forward(chunks - 1)
    finish(chunks // 2 - 1)

    for send in elem_sends:
        send.wait_send()

    def drain(chunk, carry):
        for lane in range(4):
            copy(own, 0, chunk, lane, before).wait_send()
        return carry

    lax.fori_loop(0, chunks, drain, 0)
    pltpu.make_async_copy(staged, out_hbm.at[0, :, 0], out_sem).wait()


def local(n_times, n_mom, sink_solutions, noise_sources, elementals, pairs):
    _, _, dil, width = sink_solutions.shape
    ops, _, _, nev, _ = elementals.shape
    chunks = CHUNKS
    bf16 = jnp.bfloat16
    flops = 2 * 2 * 4 * dil * width * (nev + dil) + NSEP * 2 * 4 * dil**3
    return pl.pallas_call(
        functools.partial(kernel, n_times, n_mom, chunks),
        out_shape=jax.ShapeDtypeStruct((1, NSEP, 1, 2, dil, dil), bf16),
        in_specs=[pl.BlockSpec(memory_space=pltpu.HBM)] * 4,
        out_specs=pl.BlockSpec(memory_space=pl.ANY),
        scratch_shapes=[
            pltpu.SMEM(pairs.shape, pairs.dtype),
            pltpu.VMEM((2, dil, width), bf16),
            pltpu.VMEM((dil, 2 * width), bf16),
            pltpu.VMEM((n_mom * ops, 2, nev, nev), bf16),
            pltpu.VMEM((2 * width, 2 * dil), bf16),
            pltpu.VMEM((dil, 2 * dil), bf16),
            pltpu.VMEM((2 * dil, 2 * dil), bf16),
            pltpu.VMEM((NSEP, dil, 2 * dil), bf16),
            pltpu.VMEM((NSEP, 2, dil, dil), bf16),
            pltpu.SemaphoreType.DMA((5,)),
            pltpu.SemaphoreType.DMA((max(n_mom - 1, 1),)),
            pltpu.SemaphoreType.DMA((max(n_mom - 1, 1),)),
            pltpu.SemaphoreType.DMA((4, chunks)),
            pltpu.SemaphoreType.DMA((4, chunks)),
            pltpu.SemaphoreType.DMA,
        ],
        compiler_params=pltpu.CompilerParams(
            collective_id=0, has_side_effects=True, vmem_limit_bytes=40 * 1024 * 1024
        ),
        cost_estimate=pl.CostEstimate(
            flops=flops, bytes_accessed=2 * (4 * dil * width + 8 * dil * dil), transcendentals=0
        ),
    )(
        *[
            pltpu.with_memory_space_constraint(array, pltpu.HBM)
            for array in (sink_solutions, noise_sources, elementals, pairs)
        ]
    )


def solution(mesh):
    return jax.shard_map(
        functools.partial(local, mesh.shape["tm"], mesh.shape["mom"]),
        mesh=mesh,
        in_specs=(
            P("tm", None, None, None),
            P("tm", None, None, None),
            P("mom", "tm", None, None, None),
            P("mom", None),
        ),
        out_specs=P("tm", None, "mom", None, None, None),
        check_vma=False,
    )
```

```python
import functools

import jax
import jax.numpy as jnp
from jax import lax
from jax.experimental import pallas as pl
from jax.experimental.pallas import tpu as pltpu
from jax.sharding import PartitionSpec as P

NSEP = 4
MESH = pl.DeviceIdType.MESH
CHUNKS = 16
RELAYED = 2


def dot(left, right):
    return jnp.dot(left, right, preferred_element_type=jnp.float32)


def kernel(
    n_times, n_mom, chunks,
    sink_hbm, noise_hbm, elem_hbm, pairs_hbm, out_hbm,
    pairs_ref, sink, noise, elems, weights, own, source, recv, staged, relay,
    load_sem, elem_send, elem_recv, send_sem, recv_sem, relay_send, relay_recv, out_sem,
):
    time = lax.axis_index("tm")
    mom = lax.axis_index("mom")
    odd = lax.rem(time, 2)
    upper = lax.rem(time // 2, 2)
    sibling = time + 1 - 2 * odd
    across = time + 2 - 4 * upper
    before = lax.rem(time + n_times - 4, n_times)
    after = lax.rem(time + 4, n_times)

    width = sink.shape[2]
    dil = sink.shape[1]
    ops = elem_hbm.shape[0]
    nev = elem_hbm.shape[3]
    spins = width // nev
    rows = dil // chunks

    own_elem = pltpu.make_async_copy(
        elem_hbm.at[:, 0], elems.at[pl.ds(mom * ops, ops)], load_sem.at[0]
    )
    own_elem.start()
    pairs_load = pltpu.make_async_copy(pairs_hbm, pairs_ref, load_sem.at[4])
    pairs_load.start()
    sink_load = pltpu.make_async_copy(sink_hbm.at[0], sink, load_sem.at[1])
    sink_load.start()
    noise_loads = [
        pltpu.make_async_copy(
            noise_hbm.at[0, part], noise.at[:, pl.ds(part * width, width)], load_sem.at[2 + part]
        )
        for part in range(2)
    ]
    for load in noise_loads:
        load.start()

    barrier = pltpu.get_barrier_semaphore()
    mom_peers = [lax.rem(mom + step, n_mom) for step in range(1, n_mom)]
    for peer in mom_peers:
        pl.semaphore_signal(barrier, inc=1, device_id=(time, peer), device_id_type=MESH)
    for peer in (sibling, across, before, after):
        pl.semaphore_signal(barrier, inc=1, device_id=(peer, mom), device_id_type=MESH)
    pl.semaphore_wait(barrier, n_mom - 1 + 4)

    elem_sends = []
    for step, peer in enumerate(mom_peers):
        send = pltpu.make_async_remote_copy(
            src_ref=elem_hbm.at[:, 0],
            dst_ref=elems.at[pl.ds(mom * ops, ops)],
            send_sem=elem_send.at[step],
            recv_sem=elem_recv.at[step],
            device_id=(time, peer),
            device_id_type=MESH,
        )
        send.start()
        elem_sends.append(send)
    own_elem.wait()
    pairs_load.wait()
    sink_load.wait()
    for send in elem_sends:
        send.wait_recv()
    for load in noise_loads:
        load.wait()

    def fill_weights(which):
        chosen = elems[pairs_ref[0, which]]
        real, imag = chosen[0], chosen[1]
        left = jnp.concatenate(
            [jnp.concatenate([real, -imag], axis=1), jnp.concatenate([imag, real], axis=1)], axis=0
        )
        for spin in range(spins):
            cols = pl.ds(spin * nev, nev)
            right = jnp.concatenate([sink[0, :, cols], sink[1, :, cols]], axis=1)
            applied = lax.dot_general(
                left, right, (((1,), (1,)), ((), ())), preferred_element_type=jnp.float32
            ).astype(jnp.bfloat16)
            ap_re, ap_im = applied[:nev], applied[nev:]
            upper_rows = pl.ds(spin * nev, nev)
            lower_rows = pl.ds(width + spin * nev, nev)
            weights[upper_rows, :dil] = ap_re
            weights[upper_rows, dil:] = ap_im
            weights[lower_rows, :dil] = ap_im
            weights[lower_rows, dil:] = -ap_re

    def copy(src, slot, chunk, lane, target):
        at = pl.ds(pl.multiple_of(chunk * rows, rows), rows)
        return pltpu.make_async_remote_copy(
            src_ref=src.at[at],
            dst_ref=recv.at[slot, at],
            send_sem=send_sem.at[lane, chunk],
            recv_sem=recv_sem.at[slot, chunk],
            device_id=(target, mom),
            device_id_type=MESH,
        )

    def arrived(slot, chunk):
        copy(own, slot, chunk, 0, before).wait_recv()

    fill_weights(0)

    def send_own(chunk):
        copy(own, 3, chunk, 0, before).start()

        @pl.when(upper == 1)
        def _():
            copy(own, 1, chunk, 1, across).start()

        @pl.when(odd == 1)
        def _():
            copy(own, 0, chunk, 2, sibling).start()

    first_relayed = chunks - RELAYED

    def to_relay(index):
        return pltpu.make_async_remote_copy(
            src_ref=own.at[pl.ds((first_relayed + index) * rows, rows)],
            dst_ref=relay.at[pl.ds(index * rows, rows)],
            send_sem=send_sem.at[1, first_relayed + index],
            recv_sem=relay_recv.at[index],
            device_id=(across, mom),
            device_id_type=MESH,
        )

    def from_relay(index):
        return pltpu.make_async_remote_copy(
            src_ref=relay.at[pl.ds(index * rows, rows)],
            dst_ref=recv.at[1, pl.ds((first_relayed + index) * rows, rows)],
            send_sem=relay_send.at[index],
            recv_sem=recv_sem.at[1, first_relayed + index],
            device_id=(before, mom),
            device_id_type=MESH,
        )

    per_part = 4
    tall = per_part * rows
    parts = dil // tall

    def compute_own(part):
        at = pl.ds(pl.multiple_of(part * tall, tall), tall)
        own[at, :] = dot(noise[at, :], weights[...]).astype(jnp.bfloat16)

    def make_own(part, carry):
        compute_own(part)
        for piece in range(per_part):
            send_own(part * per_part + piece)
        return carry

    make_own(0, 0)
    compute_own(parts - 1)

    @pl.when(upper == 0)
    def _():
        for index in range(RELAYED):
            to_relay(index).start()

    lax.fori_loop(1, parts - 1, make_own, 0)
    for piece in range(per_part):
        send_own((parts - 1) * per_part + piece)

    @pl.when(upper == 1)
    def _():
        for index in range(RELAYED):
            to_relay(index).wait_recv()
            from_relay(index).start()

    def make_source(part):
        at = pl.ds(pl.multiple_of(part * tall, tall), tall)
        lower = pl.ds(pl.multiple_of(dil + part * tall, tall), tall)
        meson = dot(noise[at, :], weights[...]).astype(jnp.bfloat16)
        re, im = meson[:, :dil], meson[:, dil:]
        source[at, :dil] = re
        source[at, dil:] = im
        source[lower, :dil] = -im
        source[lower, dil:] = re

    def forward(chunk):
        arrived(3, chunk)

        @pl.when((upper == 0) & (chunk < first_relayed))
        def _():
            copy(recv.at[3], 1, chunk, 1, across).start()

        @pl.when(odd == 0)
        def _():
            copy(recv.at[3], 2, chunk, 2, sibling).start()

        arrived(1, chunk)

        @pl.when(odd == 0)
        def _():
            copy(recv.at[1], 0, chunk, 3, sibling).start()

        @pl.when(odd == 1)
        def _():
            copy(recv.at[1], 2, chunk, 3, sibling).start()

    pair = 2 * rows

    def finish(part):
        at = pl.ds(pl.multiple_of(part * pair, pair), pair)
        for piece in range(2):
            arrived(0, part * 2 + piece)
            arrived(2, part * 2 + piece)
        later = recv[:, at, :].reshape(NSEP * pair, 2 * dil)
        block = dot(later, source[...]).astype(jnp.bfloat16).reshape(NSEP, pair, 2 * dil)
        staged[:, 0, at, :] = block[:, :, :dil]
        staged[:, 1, at, :] = block[:, :, dil:]
        pltpu.make_async_copy(staged.at[:, :, at], out_hbm.at[0, :, 0, :, at], out_sem).start()

    forward(0)
    fill_weights(1)

    def with_source(part, carry):
        forward(1 + part)
        make_source(part)
        return carry

    lax.fori_loop(0, 4, with_source, 0)

    def with_backlog(part, carry):
        forward(5 + part)
        finish(part)
        return carry

    lax.fori_loop(0, 4, with_backlog, 0)

    def steady(part, carry):
        forward(1 + 2 * part)
        forward(2 + 2 * part)
        finish(part)
        return carry

    lax.fori_loop(4, chunks // 2 - 1, steady, 0)
    last = chunks // 2 - 1
    at = pl.ds(last * pair, pair)

    def finish_slots(slots):
        later = jnp.concatenate([recv[slot, at, :] for slot in slots], axis=0)
        block = dot(later, source[...]).astype(jnp.bfloat16)
        for place, slot in enumerate(slots):
            mine = block[place * pair : (place + 1) * pair]
            staged[slot, 0, at, :] = mine[:, :dil]
            staged[slot, 1, at, :] = mine[:, dil:]
            pltpu.make_async_copy(
                staged.at[slot, :, at], out_hbm.at[0, slot, 0, :, at], out_sem
            ).start()

    forward(chunks - 1)
    finish_slots((1, 3))
    for piece in range(2):
        arrived(0, last * 2 + piece)
        arrived(2, last * 2 + piece)
    finish_slots((0, 2))

    for send in elem_sends:
        send.wait_send()

    def drain(chunk, carry):
        for lane in range(4):
            copy(own, 0, chunk, lane, before).wait_send()
        return carry

    lax.fori_loop(0, chunks, drain, 0)

    @pl.when(upper == 1)
    def _():
        for index in range(RELAYED):
            from_relay(index).wait_send()

    pltpu.make_async_copy(staged, out_hbm.at[0, :, 0], out_sem).wait()


def local(n_times, n_mom, sink_solutions, noise_sources, elementals, pairs):
    _, _, dil, width = sink_solutions.shape
    ops, _, _, nev, _ = elementals.shape
    chunks = CHUNKS
    bf16 = jnp.bfloat16
    flops = 2 * 2 * 4 * dil * width * (nev + dil) + NSEP * 2 * 4 * dil**3
    return pl.pallas_call(
        functools.partial(kernel, n_times, n_mom, chunks),
        out_shape=jax.ShapeDtypeStruct((1, NSEP, 1, 2, dil, dil), bf16),
        in_specs=[pl.BlockSpec(memory_space=pltpu.HBM)] * 4,
        out_specs=pl.BlockSpec(memory_space=pl.ANY),
        scratch_shapes=[
            pltpu.SMEM(pairs.shape, pairs.dtype),
            pltpu.VMEM((2, dil, width), bf16),
            pltpu.VMEM((dil, 2 * width), bf16),
            pltpu.VMEM((n_mom * ops, 2, nev, nev), bf16),
            pltpu.VMEM((2 * width, 2 * dil), bf16),
            pltpu.VMEM((dil, 2 * dil), bf16),
            pltpu.VMEM((2 * dil, 2 * dil), bf16),
            pltpu.VMEM((NSEP, dil, 2 * dil), bf16),
            pltpu.VMEM((NSEP, 2, dil, dil), bf16),
            pltpu.VMEM((RELAYED * dil // chunks, 2 * dil), bf16),
            pltpu.SemaphoreType.DMA((5,)),
            pltpu.SemaphoreType.DMA((max(n_mom - 1, 1),)),
            pltpu.SemaphoreType.DMA((max(n_mom - 1, 1),)),
            pltpu.SemaphoreType.DMA((4, chunks)),
            pltpu.SemaphoreType.DMA((4, chunks)),
            pltpu.SemaphoreType.DMA((RELAYED,)),
            pltpu.SemaphoreType.DMA((RELAYED,)),
            pltpu.SemaphoreType.DMA,
        ],
        compiler_params=pltpu.CompilerParams(
            collective_id=0, has_side_effects=True, vmem_limit_bytes=40 * 1024 * 1024
        ),
        cost_estimate=pl.CostEstimate(
            flops=flops, bytes_accessed=2 * (4 * dil * width + 8 * dil * dil), transcendentals=0
        ),
    )(
        *[
            pltpu.with_memory_space_constraint(array, pltpu.HBM)
            for array in (sink_solutions, noise_sources, elementals, pairs)
        ]
    )


def solution(mesh):
    return jax.shard_map(
        functools.partial(local, mesh.shape["tm"], mesh.shape["mom"]),
        mesh=mesh,
        in_specs=(
            P("tm", None, None, None),
            P("tm", None, None, None),
            P("mom", "tm", None, None, None),
            P("mom", None),
        ),
        out_specs=P("tm", None, "mom", None, None, None),
        check_vma=False,
    )
```
